32 devices in a mesh: tm: 16 (over z, y, core), plane: 2 (over x).
Axes of the slice: x: 2, y: 2, z: 4, core: 2. Of those that a mesh axis runs over, the one named last changes fastest.
Arguments:
- frames: bfloat16 [16, 4, 128, 256], P('tm', 'plane'), may hold values from -6 to 6
- offsets: int32 [16, 4, 2], P('tm', 'plane'), may hold values from -64 to 64
- assign: int32 [16, 4, 1, 2, 1], P('tm', 'plane'), may hold values from 0 to 1; in each aligned block of 4 rows (0 to 3, 4 to 7, ..., all dimensions but the last counted through in order) at most 4 rows name the same one
- residual: int32 [16, 4, 1, 2, 2], P('tm', 'plane'), may hold values from -8 to 8
- template: bfloat16 [4, 128, 256], P(None, None, 'plane'), may hold values from -6 to 6
Outputs:
- new_template: bfloat16 [4, 128, 256], P(None, None, 'plane')
- scores: float32 [2, 16, 4, 1, 2], P(None, 'tm', 'plane')
The draws below stay inside these ranges and needn't reach their ends.
Inputs may be any that keep to these rules, and one draw needn't show every extreme that they name: `assign`: in each aligned block of 4 rows (the patches of one volume and one plane group), no column is named more than 4 times; one column is named exactly 4 times in some block.
All inputs are finite; a program needn't handle non-finite values.
Results may differ from the reference program's by a relative error of at most 0.004.
Values may be sent and summed in bfloat16 or wider, within the bound.
A program may use at most 64 MiB of HBM per device.

```python
import math
import jax
import jax.numpy as jnp
import numpy as np
from jax import lax

PATCH = 128
GRID_R = 1
PLANE_DEV = 2
ROUNDS = 2
RES = 8
PLANES = 4
VOLS = 16
CAP = 4
N_PLANE = 2


def draw_frames(key, part):
    shape = (VOLS, PLANES, GRID_R * PATCH, N_PLANE * PATCH)
    noise_key = jax.random.fold_in(key, 11)
    pick_key = jax.random.fold_in(key, 12)
    level_key = jax.random.fold_in(key, 13)
    base = jnp.clip(jax.random.normal(noise_key, shape, jnp.float32), -6.0, 6.0)
    dimmed = jax.random.randint(pick_key, (VOLS,), 0, 2) == 1
    levels = jnp.exp(jax.random.uniform(level_key, (VOLS,), jnp.float32, math.log(0.01), math.log(0.05)))
    factor = jnp.where(dimmed, levels, jnp.ones((VOLS,), jnp.float32))
    return (base * factor[:, None, None, None]).astype(jnp.bfloat16)


def plant(result, key, low, largest):
    extent = result.shape
    spot = [jax.random.randint(jax.random.fold_in(key, axis), (), 0, extent[axis]) for axis in range(len(extent))]
    result = result.at[tuple(spot)].set(low)
    longest = extent.index(max(extent))
    spot[longest] = (spot[longest] + 1) % extent[longest]
    return result.at[tuple(spot)].set(largest)


def block_scale(own_key, shape, split, smallest, top_value):
    def one(axis_at, parts):
        heights = jax.random.uniform(jax.random.fold_in(jax.random.fold_in(own_key, 6), axis_at), (parts,), jnp.float32, smallest / len(split), top_value / len(split))
        return jnp.repeat(jnp.exp(heights), shape[axis_at] // parts).reshape((-1,) + (1,) * (len(shape) - axis_at - 1))

    factor_of = one(*split[0])
    for cut in split[1:]:
        factor_of = factor_of * one(*cut)
    return factor_of


def shared_out(rng, own, number, rows, count, top, most, slope):
    ranking = jax.random.permutation(rng, count)
    crowded, usual = portions_of(count, rows * top, most, slope, True), portions_of(count, rows * top, most, slope, False)
    places = jnp.arange(count)

    def named(sizes, offset_by):
        used = int((sizes > 0).sum())
        fixed = max(1, used // 4)
        passed = fixed + (places - fixed + offset_by * (used - fixed)) % max(1, count - fixed)
        return jnp.zeros((count,), jnp.int32).at[ranking[jnp.where(places < fixed, places, passed)]].set(jnp.asarray(sizes, jnp.int32))

    sizes = jnp.where(number % 4 == 0, named(crowded, number // 4), named(usual, number - number // 4 - 1))
    mixed = jax.random.permutation(jax.random.fold_in(own, 3), count)
    donor, sink = mixed[0:count // 2 * 2:2], mixed[1:count // 2 * 2:2]
    slack = jnp.minimum(sizes[donor] - 1, most - sizes[sink]) // 2
    slack = jnp.where((donor == ranking[0]) | (sink == ranking[0]) | (sizes[sink] == 0), 0, jnp.maximum(slack, 0))
    passed = jax.random.randint(jax.random.fold_in(own, 4), (count // 2,), 0, 1 << 20) % (slack + 1)
    sizes = sizes.at[donor].add(-passed).at[sink].add(passed)
    items = jnp.searchsorted(jnp.cumsum(sizes), jnp.arange(rows * top), side="right").astype(jnp.int32)
    listing = items.reshape(top, rows).T
    listing = listing[jax.random.permutation(jax.random.fold_in(own, 1), rows)]
    offset_by = jax.random.randint(jax.random.fold_in(own, 2), (rows, 1), 0, top)
    return jnp.take_along_axis(listing, (jnp.arange(top)[None, :] + offset_by) % top, axis=1)


def portions_of(count, total, limit, lean, full):
    portions = [(1 << 20) // math.isqrt(rank ** lean) + 1 for rank in range(1, count + 1)]
    largest = limit if full else min(limit, max(-(-total // count), total * portions[0] // sum(portions)))
    least = 1 if total - largest >= count - 1 else 0
    given, surplus = [largest] + [least] * (count - 1), total - largest - least * (count - 1)
    while surplus > 0:
        candidates = [i for i in range(1, count) if given[i] < largest] or [i for i in range(1, count) if given[i] < limit]
        mass, remaining = sum([portions[i] for i in candidates]), surplus
        for i in candidates:
            more = min(limit - given[i], max(1, remaining * portions[i] // mass), surplus)
            given[i] = given[i] + more
            surplus = surplus - more
    return np.array(given)


def centred(stream_key, dims, spread, most, pieces=(), kind=jnp.bfloat16):
    entries = spread * jax.random.normal(stream_key, dims, jnp.float32)
    if pieces:
        entries = entries * block_scale(stream_key, dims, pieces, -0.22, 0.18)
    return jnp.clip(entries, -most, most).astype(kind)


def setup_inputs(seed: int = 0) -> dict:
    key_list = jax.random.split(jax.random.key(seed), 6)
    frames = draw_frames(jax.random.fold_in(key_list[5], 71), 0)
    offsets = plant(jax.random.randint(key_list[1], (VOLS, PLANES, 2), -(PATCH // 2), PATCH // 2 + 1), jax.random.fold_in(key_list[1], 1), -(PATCH // 2), (PATCH // 2 + 1) - 1).astype(jnp.int32)
    assign_keys = jax.random.split(jax.random.fold_in(key_list[2], 1), VOLS * PLANES * GRID_R * N_PLANE // (PLANE_DEV * GRID_R * N_PLANE))
    assign_turns = jax.random.permutation(jax.random.fold_in(key_list[2], 3), VOLS * PLANES * GRID_R * N_PLANE // (PLANE_DEV * GRID_R * N_PLANE))
    assign = jax.vmap(lambda own, number: shared_out(jax.random.fold_in(key_list[2], 2), own, number, PLANE_DEV * GRID_R * N_PLANE, N_PLANE, 1, CAP, 2))(assign_keys, assign_turns).reshape((VOLS, PLANES, GRID_R, N_PLANE, 1))
    residual = plant(jax.random.randint(key_list[3], (VOLS, PLANES, GRID_R, N_PLANE, 2), -RES, RES + 1), jax.random.fold_in(key_list[3], 1), -RES, RES).astype(jnp.int32)
    template = centred(key_list[4], (PLANES, GRID_R * PATCH, N_PLANE * PATCH), 1.0, 6.0, ((2, 2),))
    return {"frames": frames, "offsets": offsets, "assign": assign, "residual": residual, "template": template}


highest = lax.Precision.HIGHEST

def dft_tables(length):
    indices = jnp.arange(length, dtype=jnp.int32)
    phases = (indices[:, None] * indices[None, :] % length).astype(jnp.float32) * (2.0 * math.pi / length)
    return (jnp.cos(phases).astype(jnp.bfloat16), jnp.sin(phases).astype(jnp.bfloat16))

def cyclic(source, amount, which_axis):
    length = source.shape[which_axis]
    doubled = jnp.concatenate([source, source], which_axis)
    return lax.dynamic_slice_in_dim(doubled, (amount % length).astype(jnp.int32), length, which_axis)

def shift_plane(frame_img, plane_off):
    return cyclic(cyclic(frame_img, plane_off[0], 0), plane_off[1], 1)

def to_tiles(tile_batch, patch_size):
    plane_count, tall, broad = tile_batch.shape
    shaped = tile_batch.reshape(plane_count, tall // patch_size, patch_size, broad // patch_size, patch_size)
    return shaped.transpose(0, 1, 3, 2, 4)

def from_tiles(tiled):
    plane_count, row_count, col_count, patch_size, patch_wide = tiled.shape
    return tiled.transpose(0, 1, 3, 2, 4).reshape(plane_count, row_count * patch_size, col_count * patch_wide)

def spectrum(tile_batch, cos_t, sin_t):
    values = tile_batch.astype(jnp.float32)
    cosine = cos_t.astype(jnp.float32)
    sine_table = sin_t.astype(jnp.float32)
    first_re = jnp.einsum('nyx,xk->nyk', values, cosine, precision=highest)
    first_im = -jnp.einsum('nyx,xk->nyk', values, sine_table, precision=highest)
    first_re = lax.optimization_barrier(first_re.astype(jnp.bfloat16)).astype(jnp.float32)
    first_im = lax.optimization_barrier(first_im.astype(jnp.bfloat16)).astype(jnp.float32)
    spec_re = jnp.einsum('uy,nyk->nuk', cosine, first_re, precision=highest) + jnp.einsum('uy,nyk->nuk', sine_table, first_im, precision=highest)
    spec_im = jnp.einsum('uy,nyk->nuk', cosine, first_im, precision=highest) - jnp.einsum('uy,nyk->nuk', sine_table, first_re, precision=highest)
    return (spec_re, spec_im)

def assess(patches, temp_re, temp_im, shift_rows, shift_cols, live_mask, cos_t, sin_t):
    patch_size = patches.shape[1]
    patch_re, patch_im = spectrum(patches, cos_t, sin_t)
    cross_re = patch_re * temp_re + patch_im * temp_im
    cross_im = patch_im * temp_re - patch_re * temp_im
    modulus = jnp.sqrt(cross_re * cross_re + cross_im * cross_im)
    levels = lax.optimization_barrier(jnp.mean(modulus, axis=(1, 2), keepdims=True))
    divisor = modulus + 0.1 * levels + 1e-06
    norm_re = lax.optimization_barrier((cross_re / divisor).astype(jnp.bfloat16)).astype(jnp.float32)
    norm_im = lax.optimization_barrier((cross_im / divisor).astype(jnp.bfloat16)).astype(jnp.float32)
    row_a = (shift_rows % patch_size).astype(jnp.int32)
    row_b = (shift_cols % patch_size).astype(jnp.int32)
    cos_a = cos_t[row_a].astype(jnp.float32)
    sin_a = sin_t[row_a].astype(jnp.float32)
    cos_b = cos_t[row_b].astype(jnp.float32)
    sin_b = sin_t[row_b].astype(jnp.float32)
    re_cos = jnp.einsum('nuv,nv->nu', norm_re, cos_b, precision=highest)
    re_sin = jnp.einsum('nuv,nv->nu', norm_re, sin_b, precision=highest)
    im_cos = jnp.einsum('nuv,nv->nu', norm_im, cos_b, precision=highest)
    im_sin = jnp.einsum('nuv,nv->nu', norm_im, sin_b, precision=highest)
    scores = (lax.optimization_barrier(jnp.sum(cos_a * re_cos, 1)) - lax.optimization_barrier(jnp.sum(sin_a * re_sin, 1)) - lax.optimization_barrier(jnp.sum(sin_a * im_cos, 1)) - lax.optimization_barrier(jnp.sum(cos_a * im_sin, 1))) / patch_size
    weights = (0.5 + jax.nn.sigmoid(scores)) * live_mask
    registered = jax.vmap(lambda single, shift_down, shift_across: cyclic(cyclic(single, shift_down, 0), shift_across, 1))(patches, shift_rows, shift_cols)
    contrib = registered.astype(jnp.float32) * weights[:, None, None]
    return (contrib, weights, scores)

def reference(frames, offsets, assign, residual, template):
    patch_size = PATCH
    rows_n = GRID_R
    cols_n = N_PLANE
    planes_n = PLANES
    cos_t, sin_t = dft_tables(patch_size)
    patch_count = planes_n * rows_n * cols_n
    plane_grid = jnp.arange(planes_n, dtype=jnp.int32)[:, None, None] * jnp.ones((1, rows_n, cols_n), jnp.int32)
    row_grid = jnp.arange(rows_n, dtype=jnp.int32)[None, :, None] * jnp.ones((planes_n, 1, cols_n), jnp.int32)
    base_index = ((plane_grid * rows_n + row_grid) * cols_n).reshape(patch_count)
    current = template
    score_list = []
    for round_index in range(ROUNDS):
        tile_stack = to_tiles(current, patch_size).reshape(patch_count, patch_size, patch_size)
        temp_re, temp_im = spectrum(tile_stack, cos_t, sin_t)

        def one_volume(carry, inputs):
            frame_img, offset_pair, owner_cols, shift_pairs = inputs
            shifted = jax.vmap(shift_plane)(frame_img, offset_pair)
            patches = to_tiles(shifted, patch_size).reshape(patch_count, patch_size, patch_size)
            target = base_index + owner_cols.reshape(patch_count).astype(jnp.int32)
            contrib, weights, scores = assess(patches, temp_re[target], temp_im[target], shift_pairs[..., 0].reshape(patch_count), shift_pairs[..., 1].reshape(patch_count), jnp.ones((patch_count,), jnp.float32), cos_t, sin_t)
            tile_sums, weight_sums = carry
            tile_sums = tile_sums.at[target].add(contrib)
            weight_sums = weight_sums.at[target].add(weights)
            return ((tile_sums, weight_sums), scores.reshape(planes_n, rows_n, cols_n))
        initial = (jnp.zeros((patch_count, patch_size, patch_size), jnp.float32), jnp.zeros((patch_count,), jnp.float32))
        (tile_sums, weight_sums), scores = lax.scan(one_volume, initial, (frames, offsets, assign, residual))
        renewed = ((tile_stack.astype(jnp.float32) + tile_sums) / (1.0 + weight_sums)[:, None, None]).astype(jnp.bfloat16)
        current = from_tiles(renewed.reshape(planes_n, rows_n, cols_n, patch_size, patch_size))
        score_list.append(scores)
    return (current, jnp.stack(score_list))
```

```python
import functools
import math

import jax
import jax.numpy as jnp
import ml_dtypes
import numpy as np
from jax import lax
from jax.experimental import pallas as pl
from jax.experimental.pallas import tpu as pltpu
from jax.sharding import PartitionSpec as P

ROUNDS = 2


highest = lax.Precision.HIGHEST


def dft_tables(length):
    indices = jnp.arange(length, dtype=jnp.int32)
    phases = (indices[:, None] * indices[None, :] % length).astype(jnp.float32) * (
        2.0 * math.pi / length
    )
    return (jnp.cos(phases).astype(jnp.bfloat16), jnp.sin(phases).astype(jnp.bfloat16))


def cyclic(source, amount, which_axis):
    length = source.shape[which_axis]
    doubled = jnp.concatenate([source, source], which_axis)
    return lax.dynamic_slice_in_dim(
        doubled, (amount % length).astype(jnp.int32), length, which_axis
    )


def shift_plane(frame_img, plane_off):
    return cyclic(cyclic(frame_img, plane_off[0], 0), plane_off[1], 1)


def to_tiles(tile_batch, patch_size):
    plane_count, tall, broad = tile_batch.shape
    shaped = tile_batch.reshape(
        plane_count, tall // patch_size, patch_size, broad // patch_size, patch_size
    )
    return shaped.transpose(0, 1, 3, 2, 4)


def spectrum(tile_batch, cos_t, sin_t):
    first_re = jnp.einsum(
        "nyx,xk->nyk", tile_batch, cos_t, preferred_element_type=jnp.float32
    ).astype(jnp.bfloat16)
    first_im = (
        -jnp.einsum("nyx,xk->nyk", tile_batch, sin_t, preferred_element_type=jnp.float32)
    ).astype(jnp.bfloat16)
    spec_re = jnp.einsum(
        "uy,nyk->nuk", cos_t, first_re, preferred_element_type=jnp.float32
    ) + jnp.einsum("uy,nyk->nuk", sin_t, first_im, preferred_element_type=jnp.float32)
    spec_im = jnp.einsum(
        "uy,nyk->nuk", cos_t, first_im, preferred_element_type=jnp.float32
    ) - jnp.einsum("uy,nyk->nuk", sin_t, first_re, preferred_element_type=jnp.float32)
    return (spec_re, spec_im)


def assess(patches, temp_re, temp_im, shift_rows, shift_cols, live_mask, cos_t, sin_t):
    patch_size = patches.shape[1]
    patch_re, patch_im = spectrum(patches, cos_t, sin_t)
    cross_re = patch_re * temp_re + patch_im * temp_im
    cross_im = patch_im * temp_re - patch_re * temp_im
    modulus = jnp.sqrt(cross_re * cross_re + cross_im * cross_im)
    levels = jnp.mean(modulus, axis=(1, 2), keepdims=True)
    divisor = modulus + 0.1 * levels + 1e-06
    norm_re = (cross_re / divisor).astype(jnp.bfloat16)
    norm_im = (cross_im / divisor).astype(jnp.bfloat16)
    row_a = (shift_rows % patch_size).astype(jnp.int32)
    row_b = (shift_cols % patch_size).astype(jnp.int32)
    cos_a = cos_t[row_a].astype(jnp.float32)
    sin_a = sin_t[row_a].astype(jnp.float32)
    cos_b = cos_t[row_b]
    sin_b = sin_t[row_b]
    re_cos = jnp.einsum("nuv,nv->nu", norm_re, cos_b, preferred_element_type=jnp.float32)
    re_sin = jnp.einsum("nuv,nv->nu", norm_re, sin_b, preferred_element_type=jnp.float32)
    im_cos = jnp.einsum("nuv,nv->nu", norm_im, cos_b, preferred_element_type=jnp.float32)
    im_sin = jnp.einsum("nuv,nv->nu", norm_im, sin_b, preferred_element_type=jnp.float32)
    scores = (
        jnp.sum(cos_a * re_cos, 1)
        - jnp.sum(sin_a * re_sin, 1)
        - jnp.sum(sin_a * im_cos, 1)
        - jnp.sum(cos_a * im_sin, 1)
    ) / patch_size
    weights = (0.5 + jax.nn.sigmoid(scores)) * live_mask
    registered = jax.vmap(
        lambda single, shift_down, shift_across: cyclic(
            cyclic(single, shift_down, 0), shift_across, 1
        )
    )(patches, shift_rows, shift_cols)
    contrib = registered.astype(jnp.float32) * weights[:, None, None]
    return (contrib, weights, scores)


def renew(old_rows_all, tile_sums, weight_sums, patch_size):
    totals, weight_all = lax.psum((tile_sums, weight_sums), "tm")
    return (
        (old_rows_all.astype(jnp.float32) + totals)
        / (1.0 + jnp.repeat(weight_all, patch_size))[:, None]
    ).astype(jnp.bfloat16)


def local(frames, offsets, assign, residual, template):
    patch_size = template.shape[2]
    planes_all = template.shape[0]
    grid_rows = template.shape[1] // patch_size
    owners = lax.axis_size("plane")
    plane_dev = frames.shape[1]
    patch_count = plane_dev * grid_rows * owners
    capacity = 2 * patch_count // owners
    plane_group = lax.axis_index("plane")
    cos_t, sin_t = dft_tables(patch_size)
    shifted = jax.vmap(shift_plane)(frames[0], offsets[0])
    patches = to_tiles(shifted, patch_size).reshape(patch_count, patch_size, patch_size)
    owner_col = assign.reshape(patch_count)
    shift_rows = residual[0, :, :, :, 0].reshape(patch_count)
    shift_cols = residual[0, :, :, :, 1].reshape(patch_count)
    counter = jnp.arange(patch_count, dtype=jnp.int32)
    plane_local = counter // (grid_rows * owners)
    row_local = counter // owners % grid_rows
    score_list = []
    column_hit = (owner_col[:, None] == jnp.arange(owners, dtype=jnp.int32)[None, :]).astype(
        jnp.int32
    )
    position = jnp.sum(jnp.cumsum(column_hit, 0) * column_hit, 1) - 1
    slot_index = owner_col * capacity + position
    slot_count = owners * capacity
    placing = slot_index[:, None] == jnp.arange(slot_count, dtype=jnp.int32)[None, :]
    outgoing = jnp.einsum(
        "rs,rxy->sxy", placing.astype(jnp.bfloat16), patches, preferred_element_type=jnp.float32
    ).astype(jnp.bfloat16)
    outgoing = outgoing.reshape(owners, capacity, patch_size, patch_size)
    details = jnp.stack(
        [
            plane_group * plane_dev + plane_local,
            row_local,
            shift_rows,
            shift_cols,
            jnp.ones_like(shift_rows),
        ],
        1,
    )
    outgoing_info = jnp.sum(placing.astype(jnp.int32)[:, :, None] * details[:, None, :], 0).reshape(
        owners, capacity, 5
    )
    current = template
    for round_index in range(ROUNDS):
        tile_stack = current
        temp_re, temp_im = spectrum(tile_stack, cos_t, sin_t)
        arrived = lax.all_to_all(outgoing, "plane", split_axis=0, concat_axis=0, tiled=True)
        arrived_info = lax.all_to_all(
            outgoing_info, "plane", split_axis=0, concat_axis=0, tiled=True
        )
        senders = arrived.shape[0]
        held_slots = arrived.shape[1]
        flat_info = arrived_info.reshape(senders * held_slots, 5)
        target = flat_info[:, 0] * grid_rows + flat_info[:, 1]
        contrib, weights, scores = assess(
            arrived.reshape(senders * held_slots, patch_size, patch_size),
            temp_re[target],
            temp_im[target],
            flat_info[:, 2],
            flat_info[:, 3],
            flat_info[:, 4].astype(jnp.float32),
            cos_t,
            sin_t,
        )
        contrib, weights, scores, target = (
            contrib.reshape(senders, held_slots, patch_size, patch_size),
            weights.reshape(senders, held_slots),
            scores.reshape(senders, held_slots),
            target.reshape(senders, held_slots),
        )
        returned = lax.all_to_all(scores, "plane", split_axis=0, concat_axis=0, tiled=True)
        score_rows = jnp.sum(placing.astype(jnp.float32) * returned.reshape(1, slot_count), 1)
        score_list.append(score_rows.reshape(plane_dev, grid_rows, owners))
        onehot = (
            target.reshape(slot_count)[:, None]
            == jnp.arange(planes_all * grid_rows, dtype=jnp.int32)[None, :]
        ).astype(jnp.float32)
        tile_sums = jnp.einsum(
            "st,sxy->txy",
            onehot,
            contrib.reshape(slot_count, patch_size, patch_size),
            precision=highest,
        )
        weight_sums = jnp.dot(weights.reshape(slot_count), onehot, precision=highest)
        renewed = renew(
            current.reshape(planes_all * grid_rows * patch_size, patch_size),
            tile_sums.reshape(planes_all * grid_rows * patch_size, patch_size),
            weight_sums,
            patch_size,
        )
        current = renewed.reshape(planes_all, grid_rows * patch_size, patch_size)
    return (current, jnp.stack(score_list)[:, None])


CHUNK = 16
MESH = pl.DeviceIdType.MESH


def trig_table(length):
    index = np.arange(length)
    phases = (index[:, None] * index[None, :] % length) * (2.0 * np.pi / length)
    return np.concatenate([np.cos(phases), np.sin(phases)], 1).astype(ml_dtypes.bfloat16)


def mxu(left, right):
    return jnp.dot(left, right, preferred_element_type=jnp.float32)


def wrapped_eye(length, amount, axis):
    near = lax.broadcasted_iota(jnp.int32, (length, length), axis)
    far = lax.broadcasted_iota(jnp.int32, (length, length), 1 - axis)
    return (((near + amount) & (length - 1)) == far).astype(jnp.float32).astype(jnp.bfloat16)


def two_stage(tile, table):
    size = tile.shape[0]
    first = mxu(tile, table)
    first_re = first[:, :size].astype(jnp.bfloat16)
    neg_re = (-first[:, :size]).astype(jnp.bfloat16)
    first_im = (-first[:, size:]).astype(jnp.bfloat16)
    stacked = jnp.concatenate(
        [
            jnp.concatenate([first_re, first_im], 1),
            jnp.concatenate([first_im, neg_re], 1),
        ],
        0,
    )
    return mxu(table, stacked)


def fused_kernel(
    n_tm, cols, plane_dev, info_ref, frames_ref, template_ref, table_ref, out_ref, scores_ref,
    temp_a, temp_b, reg_src, reg_buf, w_src, w_buf, fin, spec,
    swap_s, swap_r, reg_s, reg_r, w_s, w_r, t_s, t_r, f_s, f_r,
):
    size = table_ref.shape[0]
    chunks = size // CHUNK
    patch_count = plane_dev * cols
    me = lax.axis_index("tm")
    group = lax.axis_index("plane")
    flat = me * cols + group
    off_at, assign_at, res_at = 0, 2 * plane_dev, 2 * plane_dev + patch_count

    def place(owner):
        plane = owner // chunks
        row = pl.multiple_of((owner % chunks) * CHUNK, CHUNK)
        return plane, pl.ds(row, CHUNK)

    my_plane, my_rows = place(me)

    def around(body):
        def step(r, carry):
            body(lax.rem(me + r, n_tm))
            return carry

        lax.fori_loop(1, n_tm, step, 0)

    def across(body):
        def step(r, carry):
            body(lax.rem(group + r, cols))
            return carry

        lax.fori_loop(1, cols, step, 0)

    def everyone(body):
        def step(r, carry):
            other = lax.rem(flat + r, n_tm * cols)
            body(other, other // cols, lax.rem(other, cols))
            return carry

        lax.fori_loop(1, n_tm * cols, step, 0)

    barrier = pltpu.get_barrier_semaphore()
    around(
        lambda j: pl.semaphore_signal(barrier, inc=1, device_id=(j, group), device_id_type=MESH)
    )
    across(lambda h: pl.semaphore_signal(barrier, inc=1, device_id=(me, h), device_id_type=MESH))

    table = table_ref[...]

    patches = []
    for plane in range(plane_dev):
        frame = frames_ref[0, plane]
        rows = mxu(wrapped_eye(size, info_ref[off_at + 2 * plane], 0), frame).astype(jnp.bfloat16)
        shifted = mxu(
            rows, wrapped_eye(frame.shape[1], info_ref[off_at + 2 * plane + 1], 1)
        ).astype(jnp.bfloat16)
        for col in range(cols):
            patches.append(shifted[:, col * size : (col + 1) * size])
    for q, patch in enumerate(patches):
        rolled = mxu(wrapped_eye(size, info_ref[res_at + 2 * q], 0), patch).astype(jnp.bfloat16)
        rolled = mxu(rolled, wrapped_eye(size, info_ref[res_at + 2 * q + 1], 1))
        reg_src[q // cols, q % cols] = rolled.astype(jnp.bfloat16)

    pl.semaphore_wait(barrier, n_tm - 1 + cols - 1)

    def swap_copy(to, slot):
        return pltpu.make_async_remote_copy(
            src_ref=template_ref.at[pl.ds(to * plane_dev, plane_dev)],
            dst_ref=temp_a.at[slot],
            send_sem=swap_s.at[to],
            recv_sem=swap_r.at[slot],
            device_id=(me, to),
            device_id_type=MESH,
        )

    def reg_copy(to, slot):
        plane, rows = place(to)
        return pltpu.make_async_remote_copy(
            src_ref=reg_src.at[plane, :, rows, :],
            dst_ref=reg_buf.at[slot],
            send_sem=reg_s.at[to],
            recv_sem=reg_r.at[slot],
            device_id=(to, group),
            device_id_type=MESH,
        )

    def w_copy(k, to, slot):
        return pltpu.make_async_remote_copy(
            src_ref=w_src.at[k, to // chunks],
            dst_ref=w_buf.at[k, slot],
            send_sem=w_s.at[k, to],
            recv_sem=w_r.at[k, slot],
            device_id=(to, group),
            device_id_type=MESH,
        )

    def t_copy(to, owner):
        plane, rows = place(owner)
        return pltpu.make_async_remote_copy(
            src_ref=temp_b.at[:, plane, rows, :],
            dst_ref=temp_b.at[:, plane, rows, :],
            send_sem=t_s.at[to],
            recv_sem=t_r.at[owner],
            device_id=(to, group),
            device_id_type=MESH,
        )

    def f_copy(to, to_tm, to_plane, owner, owner_tm, owner_plane):
        plane, rows = place(owner_tm)
        return pltpu.make_async_remote_copy(
            src_ref=fin.at[to_plane],
            dst_ref=out_ref.at[owner_plane * plane_dev + plane, rows, :],
            send_sem=f_s.at[to],
            recv_sem=f_r.at[owner],
            device_id=(to_tm, to_plane),
            device_id_type=MESH,
        )

    across(lambda h: swap_copy(h, group).start())
    around(lambda j: reg_copy(j, me).start())
    temp_a[group] = template_ref[pl.ds(group * plane_dev, plane_dev)]
    reg_buf[me] = reg_src[my_plane, :, my_rows, :]

    for q, patch in enumerate(patches):
        spec[q] = two_stage(patch, table)

    row_id = lax.broadcasted_iota(jnp.int32, (2 * patch_count, size), 0)
    lane_id = lax.broadcasted_iota(jnp.int32, (2 * patch_count, size), 1)
    wanted = jnp.zeros((2 * patch_count, size), jnp.int32)
    for q in range(patch_count):
        wanted = jnp.where(row_id == q, info_ref[res_at + 2 * q], wanted)
        wanted = jnp.where(row_id == patch_count + q, info_ref[res_at + 2 * q + 1], wanted)
    onehot = ((wanted & (size - 1)) == lane_id).astype(jnp.float32).astype(jnp.bfloat16)
    picked = mxu(onehot, table)
    left = jnp.concatenate(
        [picked[:patch_count, :size], picked[:patch_count, size:]], 0
    ).astype(jnp.bfloat16)

    block_row = lax.broadcasted_iota(jnp.int32, (8, size), 0)
    across(lambda h: swap_copy(h, h).wait_recv())

    score_rows = jnp.zeros((8, size), jnp.float32)
    for k in range(ROUNDS):
        temp = temp_a if k == 0 else temp_b
        blocks = [jnp.zeros((8, size), jnp.float32) for _ in range(plane_dev)]
        for q in range(patch_count):
            plane, col = q // cols, q % cols
            target = jnp.full((size, size), info_ref[assign_at + q], jnp.int32)
            tile = temp[0, plane].astype(jnp.float32)
            for c in range(1, cols):
                tile = jnp.where(target == c, temp[c, plane].astype(jnp.float32), tile)
            temp_spec = two_stage(tile.astype(jnp.bfloat16), table)
            temp_re, temp_im = temp_spec[:, :size], temp_spec[:, size:]
            patch_re, patch_im = spec[q, :, :size], spec[q, :, size:]
            cross_re = patch_re * temp_re + patch_im * temp_im
            cross_im = patch_im * temp_re - patch_re * temp_im
            modulus = jnp.sqrt(cross_re * cross_re + cross_im * cross_im)
            level = jnp.sum(modulus, axis=0, keepdims=True)
            level = jnp.sum(level, axis=1, keepdims=True) * (1.0 / (size * size))
            inverse = 1.0 / (modulus + (0.1 * level + 1e-06))
            norm = jnp.concatenate(
                [
                    (cross_re * inverse).astype(jnp.bfloat16),
                    (cross_im * inverse).astype(jnp.bfloat16),
                ],
                1,
            )
            summed = mxu(left, norm)
            cos_row = summed[q : q + 1]
            sin_row = summed[patch_count + q : patch_count + q + 1]
            cos_b = picked[patch_count + q : patch_count + q + 1, :size]
            sin_b = picked[patch_count + q : patch_count + q + 1, size:]
            terms = (cos_row[:, :size] - sin_row[:, size:]) * cos_b - (
                sin_row[:, :size] + cos_row[:, size:]
            ) * sin_b
            score = jnp.sum(terms, axis=1, keepdims=True) * (1.0 / size)
            score = jnp.broadcast_to(score, (8, size))
            score_rows = jnp.where(block_row == k * patch_count + q, score, score_rows)
            weight = 1.0 + 0.5 * jnp.tanh(0.5 * score)
            column = jnp.full((8, size), info_ref[assign_at + q], jnp.int32)
            hit = block_row == col * cols + column
            blocks[plane] = jnp.where(hit, weight, blocks[plane])
        for plane in range(plane_dev):
            w_src[k, plane] = blocks[plane]
        around(lambda j: w_copy(k, j, me).start())
        w_buf[k, me] = w_src[k, my_plane]
        if k == 0:
            around(lambda j: reg_copy(j, j).wait_recv())
        around(lambda j: w_copy(k, j, j).wait_recv())

        sums = [temp[c, my_plane, my_rows, :].astype(jnp.float32) for c in range(cols)]
        totals = jnp.ones((8, size), jnp.float32)
        for v in range(n_tm):
            weights = w_buf[k, v]
            totals = totals + weights
            for c2 in range(cols):
                piece = reg_buf[v, c2].astype(jnp.float32)
                for c in range(cols):
                    row = c2 * cols + c
                    sums[c] = sums[c] + piece * weights[row : row + 1]
        for c in range(cols):
            total = totals[c : c + 1]
            for c2 in range(1, cols):
                total = total + (totals[c2 * cols + c : c2 * cols + c + 1] - 1.0)
            fresh = (sums[c] / total).astype(jnp.bfloat16)
            if k < ROUNDS - 1:
                temp_b[c, my_plane, my_rows, :] = fresh
            else:
                fin[c] = fresh
        if k < ROUNDS - 1:
            around(lambda j: t_copy(j, me).start())
            around(lambda j: t_copy(j, j).wait_recv())

    everyone(lambda d, j, h: f_copy(d, j, h, flat, me, group).start())
    out_ref[group * plane_dev + my_plane, my_rows, :] = fin[group]
    scores_ref[...] = score_rows
    across(lambda h: swap_copy(h, group).wait_send())
    around(lambda j: reg_copy(j, me).wait_send())
    for k in range(ROUNDS):
        around(lambda j: w_copy(k, j, me).wait_send())
    around(lambda j: t_copy(j, me).wait_send())
    everyone(lambda d, j, h: f_copy(d, j, h, d, j, h).wait_recv())
    everyone(lambda d, j, h: f_copy(d, j, h, flat, me, group).wait_send())


def fused(n_tm, cols, frames, offsets, assign, residual, template):
    plane_dev = frames.shape[1]
    size = template.shape[2]
    patch_count = plane_dev * cols
    info = jnp.concatenate([offsets.reshape(-1), assign.reshape(-1), residual.reshape(-1)])
    vmem = pl.BlockSpec(memory_space=pltpu.VMEM)
    dma = pltpu.SemaphoreType.DMA
    out, scores = pl.pallas_call(
        functools.partial(fused_kernel, n_tm, cols, plane_dev),
        out_shape=(
            jax.ShapeDtypeStruct(template.shape, jnp.bfloat16),
            jax.ShapeDtypeStruct((8, size), jnp.float32),
        ),
        in_specs=[pl.BlockSpec(memory_space=pltpu.SMEM), vmem, vmem, vmem],
        out_specs=(vmem, vmem),
        scratch_shapes=[
            pltpu.VMEM((cols, plane_dev, size, size), jnp.bfloat16),
            pltpu.VMEM((cols, plane_dev, size, size), jnp.bfloat16),
            pltpu.VMEM((plane_dev, cols, size, size), jnp.bfloat16),
            pltpu.VMEM((n_tm, cols, CHUNK, size), jnp.bfloat16),
            pltpu.VMEM((ROUNDS, plane_dev, 8, size), jnp.float32),
            pltpu.VMEM((ROUNDS, n_tm, 8, size), jnp.float32),
            pltpu.VMEM((cols, CHUNK, size), jnp.bfloat16),
            pltpu.VMEM((patch_count, size, 2 * size), jnp.float32),
            dma((cols,)),
            dma((cols,)),
            dma((n_tm,)),
            dma((n_tm,)),
            dma((ROUNDS, n_tm)),
            dma((ROUNDS, n_tm)),
            dma((n_tm,)),
            dma((n_tm,)),
            dma((n_tm * cols,)),
            dma((n_tm * cols,)),
        ],
        compiler_params=pltpu.CompilerParams(
            collective_id=0, has_side_effects=True, vmem_limit_bytes=16 * 1024 * 1024
        ),
    )(info, frames, template, jnp.asarray(trig_table(size)))
    scores = scores[: ROUNDS * patch_count, 0].reshape(ROUNDS, 1, plane_dev, 1, cols)
    return out, scores


def dispatch(n_tm, cols, frames, offsets, assign, residual, template):
    size = template.shape[2]
    plane_dev = frames.shape[1]
    width = frames.shape[3]
    fits = (
        plane_dev * size == n_tm * CHUNK
        and template.shape[1] == size
        and cols * cols <= 8
        and ROUNDS * plane_dev * cols <= 8
        and size & (size - 1) == 0
        and width & (width - 1) == 0
        and size % 128 == 0
    )
    if fits:
        return fused(n_tm, cols, frames, offsets, assign, residual, template)
    return local(frames, offsets, assign, residual, template)


def solution(mesh):
    return jax.shard_map(
        functools.partial(dispatch, mesh.shape["tm"], mesh.shape["plane"]),
        mesh=mesh,
        in_specs=(
            P("tm", "plane", None, None),
            P("tm", "plane", None),
            P("tm", "plane", None, None, None),
            P("tm", "plane", None, None, None),
            P(None, None, "plane"),
        ),
        out_specs=(P(None, None, "plane"), P(None, "tm", "plane", None, None)),
        check_vma=False,
    )
```

```python
import functools
import math

import jax
import jax.numpy as jnp
import ml_dtypes
import numpy as np
from jax import lax
from jax.experimental import pallas as pl
from jax.experimental.pallas import tpu as pltpu
from jax.sharding import PartitionSpec as P

ROUNDS = 2


highest = lax.Precision.HIGHEST


def dft_tables(length):
    indices = jnp.arange(length, dtype=jnp.int32)
    phases = (indices[:, None] * indices[None, :] % length).astype(jnp.float32) * (
        2.0 * math.pi / length
    )
    return (jnp.cos(phases).astype(jnp.bfloat16), jnp.sin(phases).astype(jnp.bfloat16))


def cyclic(source, amount, which_axis):
    length = source.shape[which_axis]
    doubled = jnp.concatenate([source, source], which_axis)
    return lax.dynamic_slice_in_dim(
        doubled, (amount % length).astype(jnp.int32), length, which_axis
    )


def shift_plane(frame_img, plane_off):
    return cyclic(cyclic(frame_img, plane_off[0], 0), plane_off[1], 1)


def to_tiles(tile_batch, patch_size):
    plane_count, tall, broad = tile_batch.shape
    shaped = tile_batch.reshape(
        plane_count, tall // patch_size, patch_size, broad // patch_size, patch_size
    )
    return shaped.transpose(0, 1, 3, 2, 4)


def spectrum(tile_batch, cos_t, sin_t):
    first_re = jnp.einsum(
        "nyx,xk->nyk", tile_batch, cos_t, preferred_element_type=jnp.float32
    ).astype(jnp.bfloat16)
    first_im = (
        -jnp.einsum("nyx,xk->nyk", tile_batch, sin_t, preferred_element_type=jnp.float32)
    ).astype(jnp.bfloat16)
    spec_re = jnp.einsum(
        "uy,nyk->nuk", cos_t, first_re, preferred_element_type=jnp.float32
    ) + jnp.einsum("uy,nyk->nuk", sin_t, first_im, preferred_element_type=jnp.float32)
    spec_im = jnp.einsum(
        "uy,nyk->nuk", cos_t, first_im, preferred_element_type=jnp.float32
    ) - jnp.einsum("uy,nyk->nuk", sin_t, first_re, preferred_element_type=jnp.float32)
    return (spec_re, spec_im)


def assess(patches, temp_re, temp_im, shift_rows, shift_cols, live_mask, cos_t, sin_t):
    patch_size = patches.shape[1]
    patch_re, patch_im = spectrum(patches, cos_t, sin_t)
    cross_re = patch_re * temp_re + patch_im * temp_im
    cross_im = patch_im * temp_re - patch_re * temp_im
    modulus = jnp.sqrt(cross_re * cross_re + cross_im * cross_im)
    levels = jnp.mean(modulus, axis=(1, 2), keepdims=True)
    divisor = modulus + 0.1 * levels + 1e-06
    norm_re = (cross_re / divisor).astype(jnp.bfloat16)
    norm_im = (cross_im / divisor).astype(jnp.bfloat16)
    row_a = (shift_rows % patch_size).astype(jnp.int32)
    row_b = (shift_cols % patch_size).astype(jnp.int32)
    cos_a = cos_t[row_a].astype(jnp.float32)
    sin_a = sin_t[row_a].astype(jnp.float32)
    cos_b = cos_t[row_b]
    sin_b = sin_t[row_b]
    re_cos = jnp.einsum("nuv,nv->nu", norm_re, cos_b, preferred_element_type=jnp.float32)
    re_sin = jnp.einsum("nuv,nv->nu", norm_re, sin_b, preferred_element_type=jnp.float32)
    im_cos = jnp.einsum("nuv,nv->nu", norm_im, cos_b, preferred_element_type=jnp.float32)
    im_sin = jnp.einsum("nuv,nv->nu", norm_im, sin_b, preferred_element_type=jnp.float32)
    scores = (
        jnp.sum(cos_a * re_cos, 1)
        - jnp.sum(sin_a * re_sin, 1)
        - jnp.sum(sin_a * im_cos, 1)
        - jnp.sum(cos_a * im_sin, 1)
    ) / patch_size
    weights = (0.5 + jax.nn.sigmoid(scores)) * live_mask
    registered = jax.vmap(
        lambda single, shift_down, shift_across: cyclic(
            cyclic(single, shift_down, 0), shift_across, 1
        )
    )(patches, shift_rows, shift_cols)
    contrib = registered.astype(jnp.float32) * weights[:, None, None]
    return (contrib, weights, scores)


def renew(old_rows_all, tile_sums, weight_sums, patch_size):
    totals, weight_all = lax.psum((tile_sums, weight_sums), "tm")
    return (
        (old_rows_all.astype(jnp.float32) + totals)
        / (1.0 + jnp.repeat(weight_all, patch_size))[:, None]
    ).astype(jnp.bfloat16)


def local(frames, offsets, assign, residual, template):
    patch_size = template.shape[2]
    planes_all = template.shape[0]
    grid_rows = template.shape[1] // patch_size
    owners = lax.axis_size("plane")
    plane_dev = frames.shape[1]
    patch_count = plane_dev * grid_rows * owners
    capacity = 2 * patch_count // owners
    plane_group = lax.axis_index("plane")
    cos_t, sin_t = dft_tables(patch_size)
    shifted = jax.vmap(shift_plane)(frames[0], offsets[0])
    patches = to_tiles(shifted, patch_size).reshape(patch_count, patch_size, patch_size)
    owner_col = assign.reshape(patch_count)
    shift_rows = residual[0, :, :, :, 0].reshape(patch_count)
    shift_cols = residual[0, :, :, :, 1].reshape(patch_count)
    counter = jnp.arange(patch_count, dtype=jnp.int32)
    plane_local = counter // (grid_rows * owners)
    row_local = counter // owners % grid_rows
    score_list = []
    column_hit = (owner_col[:, None] == jnp.arange(owners, dtype=jnp.int32)[None, :]).astype(
        jnp.int32
    )
    position = jnp.sum(jnp.cumsum(column_hit, 0) * column_hit, 1) - 1
    slot_index = owner_col * capacity + position
    slot_count = owners * capacity
    placing = slot_index[:, None] == jnp.arange(slot_count, dtype=jnp.int32)[None, :]
    outgoing = jnp.einsum(
        "rs,rxy->sxy", placing.astype(jnp.bfloat16), patches, preferred_element_type=jnp.float32
    ).astype(jnp.bfloat16)
    outgoing = outgoing.reshape(owners, capacity, patch_size, patch_size)
    details = jnp.stack(
        [
            plane_group * plane_dev + plane_local,
            row_local,
            shift_rows,
            shift_cols,
            jnp.ones_like(shift_rows),
        ],
        1,
    )
    outgoing_info = jnp.sum(placing.astype(jnp.int32)[:, :, None] * details[:, None, :], 0).reshape(
        owners, capacity, 5
    )
    current = template
    for round_index in range(ROUNDS):
        tile_stack = current
        temp_re, temp_im = spectrum(tile_stack, cos_t, sin_t)
        arrived = lax.all_to_all(outgoing, "plane", split_axis=0, concat_axis=0, tiled=True)
        arrived_info = lax.all_to_all(
            outgoing_info, "plane", split_axis=0, concat_axis=0, tiled=True
        )
        senders = arrived.shape[0]
        held_slots = arrived.shape[1]
        flat_info = arrived_info.reshape(senders * held_slots, 5)
        target = flat_info[:, 0] * grid_rows + flat_info[:, 1]
        contrib, weights, scores = assess(
            arrived.reshape(senders * held_slots, patch_size, patch_size),
            temp_re[target],
            temp_im[target],
            flat_info[:, 2],
            flat_info[:, 3],
            flat_info[:, 4].astype(jnp.float32),
            cos_t,
            sin_t,
        )
        contrib, weights, scores, target = (
            contrib.reshape(senders, held_slots, patch_size, patch_size),
            weights.reshape(senders, held_slots),
            scores.reshape(senders, held_slots),
            target.reshape(senders, held_slots),
        )
        returned = lax.all_to_all(scores, "plane", split_axis=0, concat_axis=0, tiled=True)
        score_rows = jnp.sum(placing.astype(jnp.float32) * returned.reshape(1, slot_count), 1)
        score_list.append(score_rows.reshape(plane_dev, grid_rows, owners))
        onehot = (
            target.reshape(slot_count)[:, None]
            == jnp.arange(planes_all * grid_rows, dtype=jnp.int32)[None, :]
        ).astype(jnp.float32)
        tile_sums = jnp.einsum(
            "st,sxy->txy",
            onehot,
            contrib.reshape(slot_count, patch_size, patch_size),
            precision=highest,
        )
        weight_sums = jnp.dot(weights.reshape(slot_count), onehot, precision=highest)
        renewed = renew(
            current.reshape(planes_all * grid_rows * patch_size, patch_size),
            tile_sums.reshape(planes_all * grid_rows * patch_size, patch_size),
            weight_sums,
            patch_size,
        )
        current = renewed.reshape(planes_all, grid_rows * patch_size, patch_size)
    return (current, jnp.stack(score_list)[:, None])


REPLICAS = 2
CHUNK = 16 * REPLICAS
MESH = pl.DeviceIdType.MESH


def trig_table(length):
    index = np.arange(length)
    phases = (index[:, None] * index[None, :] % length) * (2.0 * np.pi / length)
    return np.concatenate([np.cos(phases), np.sin(phases)], 1).astype(ml_dtypes.bfloat16)


def mxu(left, right):
    return jnp.dot(left, right, preferred_element_type=jnp.float32)


def wrapped_eye(length, amount, axis):
    near = lax.broadcasted_iota(jnp.int32, (length, length), axis)
    far = lax.broadcasted_iota(jnp.int32, (length, length), 1 - axis)
    return (((near + amount) & (length - 1)) == far).astype(jnp.float32).astype(jnp.bfloat16)


def two_stage(tile, table):
    size = tile.shape[0]
    first = mxu(tile, table)
    first_re = first[:, :size].astype(jnp.bfloat16)
    neg_re = (-first[:, :size]).astype(jnp.bfloat16)
    first_im = (-first[:, size:]).astype(jnp.bfloat16)
    stacked = jnp.concatenate(
        [
            jnp.concatenate([first_re, first_im], 1),
            jnp.concatenate([first_im, neg_re], 1),
        ],
        0,
    )
    return mxu(table, stacked)


def fused_kernel(
    n_tm, cols, plane_dev, offsets_ref, assign_ref, residual_ref, frames_hbm, template_ref, table_hbm,
    out_ref, scores_ref, frames_ref, table_ref, load_s, temp_a, temp_b, reg_src, reg_buf, w_src, w_buf, fin, spec,
    swap_s, swap_r, reg_s, reg_r, w_s, w_r, t_s, t_r, f_s, f_r,
):
    size = table_ref.shape[0]
    chunks = size // CHUNK
    patch_count = plane_dev * cols
    me = lax.axis_index("tm")
    group = lax.axis_index("plane")
    units = n_tm // REPLICAS
    unit = lax.rem(me, units)
    base = me - unit
    flat = unit * cols + group
    assigned = [assign_ref[q // cols, 0, q % cols] for q in range(patch_count)]
    down = [residual_ref[q // cols, q % cols, 0] for q in range(patch_count)]
    across_by = [residual_ref[q // cols, q % cols, 1] for q in range(patch_count)]

    def place(owner):
        owner = lax.rem(owner, units)
        plane = lax.div(owner, chunks)
        row = pl.multiple_of(lax.rem(owner, chunks) * CHUNK, CHUNK)
        return plane, pl.ds(row, CHUNK)

    my_plane, my_rows = place(me)

    def around(body):
        def step(r, carry):
            body(lax.rem(me + r, n_tm))
            return carry

        lax.fori_loop(1, n_tm, step, 0)

    def replica(body):
        def step(r, carry):
            body(lax.rem(unit + r, units))
            return carry

        lax.fori_loop(1, units, step, 0)

    def owners_of(plane, first, count, body):
        def step(r, carry):
            owner = plane * chunks + lax.rem(unit + r, chunks)
            for part in range(count):
                device = first + part * units + owner
                pl.when(device != me)(functools.partial(body, device))
            return carry

        lax.fori_loop(0, chunks, step, 0)

    def across(body):
        def step(r, carry):
            body(lax.rem(group + r, cols))
            return carry

        lax.fori_loop(1, cols, step, 0)

    def everyone(body):
        def step(r, carry):
            other = lax.rem(flat + r, units * cols)
            body(other, lax.div(other, cols), lax.rem(other, cols))
            return carry

        lax.fori_loop(1, units * cols, step, 0)

    frames_load = pltpu.make_async_copy(frames_hbm.at[0], frames_ref, load_s.at[0])
    table_load = pltpu.make_async_copy(table_hbm, table_ref, load_s.at[1])
    own_load = pltpu.make_async_copy(
        template_ref.at[pl.ds(group * plane_dev, plane_dev)], temp_a.at[group], load_s.at[2]
    )
    frames_load.start()
    table_load.start()
    own_load.start()

    barrier = pltpu.get_barrier_semaphore()
    around(
        lambda j: pl.semaphore_signal(barrier, inc=1, device_id=(j, group), device_id_type=MESH)
    )
    across(lambda h: pl.semaphore_signal(barrier, inc=1, device_id=(me, h), device_id_type=MESH))

    frames_load.wait()

    patches = []
    for plane in range(plane_dev):
        frame = frames_ref[plane]
        rows = mxu(wrapped_eye(size, offsets_ref[plane, 0], 0), frame).astype(jnp.bfloat16)
        shifted = mxu(
            rows, wrapped_eye(frame.shape[1], offsets_ref[plane, 1], 1)
        ).astype(jnp.bfloat16)
        for col in range(cols):
            patches.append(shifted[:, col * size : (col + 1) * size])
    pl.semaphore_wait(barrier, n_tm - 1 + cols - 1)

    def swap_copy(to, slot):
        return pltpu.make_async_remote_copy(
            src_ref=template_ref.at[pl.ds(to * plane_dev, plane_dev)],
            dst_ref=temp_a.at[slot],
            send_sem=swap_s.at[to],
            recv_sem=swap_r.at[slot],
            device_id=(me, to),
            device_id_type=MESH,
        )

    def reg_copy(to, slot):
        plane, rows = place(to)
        return pltpu.make_async_remote_copy(
            src_ref=reg_src.at[plane, :, rows, :],
            dst_ref=reg_buf.at[slot],
            send_sem=reg_s.at[to],
            recv_sem=reg_r.at[slot],
            device_id=(to, group),
            device_id_type=MESH,
        )

    def w_copy(k, to, slot):
        return pltpu.make_async_remote_copy(
            src_ref=w_src.at[k, lax.div(lax.rem(to, units), chunks)],
            dst_ref=w_buf.at[k, slot],
            send_sem=w_s.at[k, to],
            recv_sem=w_r.at[k, slot],
            device_id=(to, group),
            device_id_type=MESH,
        )

    def t_copy(to, owner):
        plane, rows = place(owner)
        return pltpu.make_async_remote_copy(
            src_ref=temp_b.at[:, plane, rows, :],
            dst_ref=temp_b.at[:, plane, rows, :],
            send_sem=t_s.at[to],
            recv_sem=t_r.at[owner],
            device_id=(base + to, group),
            device_id_type=MESH,
        )

    def f_copy(to, to_tm, to_plane, owner, owner_tm, owner_plane):
        plane, rows = place(owner_tm)
        return pltpu.make_async_remote_copy(
            src_ref=fin.at[to_plane],
            dst_ref=out_ref.at[owner_plane * plane_dev + plane, rows, :],
            send_sem=f_s.at[to],
            recv_sem=f_r.at[owner],
            device_id=(base + to_tm, to_plane),
            device_id_type=MESH,
        )

    across(lambda h: swap_copy(h, group).start())
    table_load.wait()
    table = table_ref[...].astype(jnp.bfloat16)
    for q, patch in enumerate(patches):
        rolled = mxu(wrapped_eye(size, down[q], 0), patch).astype(jnp.bfloat16)
        rolled = mxu(rolled, wrapped_eye(size, across_by[q], 1))
        reg_src[q // cols, q % cols] = rolled.astype(jnp.bfloat16)
    around(lambda j: reg_copy(j, me).start())
    reg_buf[me] = reg_src[my_plane, :, my_rows, :]
    for q, patch in enumerate(patches):
        spec[q] = two_stage(patch, table)

    row_id = lax.broadcasted_iota(jnp.int32, (2 * patch_count, size), 0)
    lane_id = lax.broadcasted_iota(jnp.int32, (2 * patch_count, size), 1)
    wanted = jnp.zeros((2 * patch_count, size), jnp.int32)
    for q in range(patch_count):
        wanted = jnp.where(row_id == q, down[q], wanted)
        wanted = jnp.where(row_id == patch_count + q, across_by[q], wanted)
    onehot = ((wanted & (size - 1)) == lane_id).astype(jnp.float32).astype(jnp.bfloat16)
    picked = mxu(onehot, table)
    left = jnp.concatenate(
        [picked[:patch_count, :size], picked[:patch_count, size:]], 0
    ).astype(jnp.bfloat16)

    own_load.wait()
    across(lambda h: swap_copy(h, h).wait_recv())

    lane_at = lax.broadcasted_iota(jnp.int32, (1, size), 1)
    for k in range(ROUNDS):
        temp = temp_a if k == 0 else temp_b
        for q in range(patch_count):
            plane, col = q // cols, q % cols
            if col == 0:
                score_row = jnp.zeros((1, size), jnp.float32)
                weight_row = jnp.zeros((1, size), jnp.float32)
                if k > 0:
                    owners_of(plane, base, 1, lambda j: t_copy(j - base, j - base).wait_recv())
            target = jnp.full((size, size), assigned[q], jnp.int32)
            tile = temp[0, plane].astype(jnp.float32)
            for c in range(1, cols):
                tile = jnp.where(target == c, temp[c, plane].astype(jnp.float32), tile)
            temp_spec = two_stage(tile.astype(jnp.bfloat16), table)
            temp_re, temp_im = temp_spec[:, :size], temp_spec[:, size:]
            patch_re, patch_im = spec[q, :, :size], spec[q, :, size:]
            cross_re = patch_re * temp_re + patch_im * temp_im
            cross_im = patch_im * temp_re - patch_re * temp_im
            modulus = jnp.sqrt(cross_re * cross_re + cross_im * cross_im)
            level = jnp.sum(modulus, axis=0, keepdims=True)
            level = jnp.sum(level, axis=1, keepdims=True) * (1.0 / (size * size))
            inverse = 1.0 / (modulus + (0.1 * level + 1e-06))
            norm = jnp.concatenate(
                [
                    (cross_re * inverse).astype(jnp.bfloat16),
                    (cross_im * inverse).astype(jnp.bfloat16),
                ],
                1,
            )
            summed = mxu(left, norm)
            cos_row = summed[q : q + 1]
            sin_row = summed[patch_count + q : patch_count + q + 1]
            cos_b = picked[patch_count + q : patch_count + q + 1, :size]
            sin_b = picked[patch_count + q : patch_count + q + 1, size:]
            terms = (cos_row[:, :size] - sin_row[:, size:]) * cos_b - (
                sin_row[:, :size] + cos_row[:, size:]
            ) * sin_b
            score = jnp.sum(terms, axis=1, keepdims=True) * (1.0 / size)
            score = jnp.broadcast_to(score, (8, size))[:1]
            score_row = jnp.where(lane_at == col, score, score_row)
            weight = 1.0 + 0.5 * jnp.tanh(0.5 * score)
            target_row = jnp.full((1, size), assigned[q], jnp.int32)
            weight_row = jnp.where(lane_at == col * cols + target_row, weight, weight_row)
            if col == cols - 1:
                w_src[k, plane] = weight_row
                owners_of(plane, 0, REPLICAS, lambda j: w_copy(k, j, me).start())
                scores_ref[k, 0, plane] = score_row[:, :cols]
        w_buf[k, me] = w_src[k, my_plane]
        if k == 0:
            around(lambda j: reg_copy(j, j).wait_recv())
        around(lambda j: w_copy(k, j, j).wait_recv())

        sums = [temp[c, my_plane, my_rows, :].astype(jnp.float32) for c in range(cols)]
        lanes = lax.broadcasted_iota(jnp.int32, (n_tm, size), 1)
        gathered = w_buf[k].reshape(n_tm, size)
        spread = [
            jnp.broadcast_to(
                jnp.sum(jnp.where(lanes == row, gathered, 0.0), axis=1, keepdims=True),
                (n_tm, size),
            )
            for row in range(cols * cols)
        ]
        for v in range(n_tm):
            for c2 in range(cols):
                piece = reg_buf[v, c2].astype(jnp.float32)
                for c in range(cols):
                    sums[c] = sums[c] + piece * spread[c2 * cols + c][v : v + 1]
        for c in range(cols):
            weights = spread[c]
            for c2 in range(1, cols):
                weights = weights + spread[c2 * cols + c]
            total = 1.0 + jnp.sum(weights, axis=0, keepdims=True)
            fresh = (sums[c] / total).astype(jnp.bfloat16)
            if k < ROUNDS - 1:
                temp_b[c, my_plane, my_rows, :] = fresh
            else:
                fin[c] = fresh
        if k < ROUNDS - 1:
            replica(lambda u: t_copy(u, unit).start())

    everyone(lambda d, j, h: f_copy(d, j, h, flat, unit, group).start())
    own_store = pltpu.make_async_copy(
        fin.at[group], out_ref.at[group * plane_dev + my_plane, my_rows, :], load_s.at[3]
    )
    own_store.start()
    across(lambda h: swap_copy(h, group).wait_send())
    around(lambda j: reg_copy(j, me).wait_send())
    for k in range(ROUNDS):
        around(lambda j: w_copy(k, j, me).wait_send())
    replica(lambda u: t_copy(u, unit).wait_send())
    own_store.wait()
    everyone(lambda d, j, h: f_copy(d, j, h, d, j, h).wait_recv())
    everyone(lambda d, j, h: f_copy(d, j, h, flat, unit, group).wait_send())


def fused(n_tm, cols, frames, offsets, assign, residual, template):
    plane_dev = frames.shape[1]
    size = template.shape[2]
    patch_count = plane_dev * cols
    vmem = pl.BlockSpec(memory_space=pltpu.VMEM)
    smem = pl.BlockSpec(memory_space=pltpu.SMEM)
    hbm = pl.BlockSpec(memory_space=pltpu.HBM)
    dma = pltpu.SemaphoreType.DMA
    return pl.pallas_call(
        functools.partial(fused_kernel, n_tm, cols, plane_dev),
        out_shape=(
            jax.ShapeDtypeStruct(template.shape, jnp.bfloat16),
            jax.ShapeDtypeStruct((ROUNDS, 1, plane_dev, 1, cols), jnp.float32),
        ),
        in_specs=[smem, smem, smem, hbm, hbm, hbm],
        out_specs=(hbm, vmem),
        scratch_shapes=[
            pltpu.VMEM(frames.shape[1:], jnp.bfloat16),
            pltpu.VMEM((size, 2 * size), jnp.float32),
            dma((4,)),
            pltpu.VMEM((cols, plane_dev, size, size), jnp.bfloat16),
            pltpu.VMEM((cols, plane_dev, size, size), jnp.bfloat16),
            pltpu.VMEM((plane_dev, cols, size, size), jnp.bfloat16),
            pltpu.VMEM((n_tm, cols, CHUNK, size), jnp.bfloat16),
            pltpu.VMEM((ROUNDS, plane_dev, 1, size), jnp.float32),
            pltpu.VMEM((ROUNDS, n_tm, 1, size), jnp.float32),
            pltpu.VMEM((cols, CHUNK, size), jnp.bfloat16),
            pltpu.VMEM((patch_count, size, 2 * size), jnp.float32),
            dma((cols,)),
            dma((cols,)),
            dma((n_tm,)),
            dma((n_tm,)),
            dma((ROUNDS, n_tm)),
            dma((ROUNDS, n_tm)),
            dma((n_tm // REPLICAS,)),
            dma((n_tm // REPLICAS,)),
            dma((n_tm // REPLICAS * cols,)),
            dma((n_tm // REPLICAS * cols,)),
        ],
        compiler_params=pltpu.CompilerParams(
            collective_id=0, has_side_effects=True
        ),
    )(
        offsets.reshape(plane_dev, 2),
        assign.reshape(plane_dev, 1, cols),
        residual.reshape(plane_dev, cols, 2),
        frames,
        template,
        jnp.asarray(trig_table(size).astype(np.float32)),
    )


def dispatch(n_tm, cols, frames, offsets, assign, residual, template):
    size = template.shape[2]
    plane_dev = frames.shape[1]
    width = frames.shape[3]
    fits = (
        n_tm % REPLICAS == 0
        and plane_dev * size == n_tm // REPLICAS * CHUNK
        and template.shape[1] == size
        and cols * cols <= 8
        and 2 * plane_dev * cols <= 8
        and size & (size - 1) == 0
        and width & (width - 1) == 0
        and size % 128 == 0
    )
    if fits:
        return fused(n_tm, cols, frames, offsets, assign, residual, template)
    return local(frames, offsets, assign, residual, template)


def solution(mesh):
    return jax.shard_map(
        functools.partial(dispatch, mesh.shape["tm"], mesh.shape["plane"]),
        mesh=mesh,
        in_specs=(
            P("tm", "plane", None, None),
            P("tm", "plane", None),
            P("tm", "plane", None, None, None),
            P("tm", "plane", None, None, None),
            P(None, None, "plane"),
        ),
        out_specs=(P(None, None, "plane"), P(None, "tm", "plane", None, None)),
        check_vma=False,
    )
```

```python
import functools
import math

import jax
import jax.numpy as jnp
import ml_dtypes
import numpy as np
from jax import lax
from jax.experimental import pallas as pl
from jax.experimental.pallas import tpu as pltpu
from jax.sharding import PartitionSpec as P

ROUNDS = 2


highest = lax.Precision.HIGHEST


def dft_tables(length):
    indices = jnp.arange(length, dtype=jnp.int32)
    phases = (indices[:, None] * indices[None, :] % length).astype(jnp.float32) * (
        2.0 * math.pi / length
    )
    return (jnp.cos(phases).astype(jnp.bfloat16), jnp.sin(phases).astype(jnp.bfloat16))


def cyclic(source, amount, which_axis):
    length = source.shape[which_axis]
    doubled = jnp.concatenate([source, source], which_axis)
    return lax.dynamic_slice_in_dim(
        doubled, (amount % length).astype(jnp.int32), length, which_axis
    )


def shift_plane(frame_img, plane_off):
    return cyclic(cyclic(frame_img, plane_off[0], 0), plane_off[1], 1)


def to_tiles(tile_batch, patch_size):
    plane_count, tall, broad = tile_batch.shape
    shaped = tile_batch.reshape(
        plane_count, tall // patch_size, patch_size, broad // patch_size, patch_size
    )
    return shaped.transpose(0, 1, 3, 2, 4)


def spectrum(tile_batch, cos_t, sin_t):
    first_re = jnp.einsum(
        "nyx,xk->nyk", tile_batch, cos_t, preferred_element_type=jnp.float32
    ).astype(jnp.bfloat16)
    first_im = (
        -jnp.einsum("nyx,xk->nyk", tile_batch, sin_t, preferred_element_type=jnp.float32)
    ).astype(jnp.bfloat16)
    spec_re = jnp.einsum(
        "uy,nyk->nuk", cos_t, first_re, preferred_element_type=jnp.float32
    ) + jnp.einsum("uy,nyk->nuk", sin_t, first_im, preferred_element_type=jnp.float32)
    spec_im = jnp.einsum(
        "uy,nyk->nuk", cos_t, first_im, preferred_element_type=jnp.float32
    ) - jnp.einsum("uy,nyk->nuk", sin_t, first_re, preferred_element_type=jnp.float32)
    return (spec_re, spec_im)


def assess(patches, temp_re, temp_im, shift_rows, shift_cols, live_mask, cos_t, sin_t):
    patch_size = patches.shape[1]
    patch_re, patch_im = spectrum(patches, cos_t, sin_t)
    cross_re = patch_re * temp_re + patch_im * temp_im
    cross_im = patch_im * temp_re - patch_re * temp_im
    modulus = jnp.sqrt(cross_re * cross_re + cross_im * cross_im)
    levels = jnp.mean(modulus, axis=(1, 2), keepdims=True)
    divisor = modulus + 0.1 * levels + 1e-06
    norm_re = (cross_re / divisor).astype(jnp.bfloat16)
    norm_im = (cross_im / divisor).astype(jnp.bfloat16)
    row_a = (shift_rows % patch_size).astype(jnp.int32)
    row_b = (shift_cols % patch_size).astype(jnp.int32)
    cos_a = cos_t[row_a].astype(jnp.float32)
    sin_a = sin_t[row_a].astype(jnp.float32)
    cos_b = cos_t[row_b]
    sin_b = sin_t[row_b]
    re_cos = jnp.einsum("nuv,nv->nu", norm_re, cos_b, preferred_element_type=jnp.float32)
    re_sin = jnp.einsum("nuv,nv->nu", norm_re, sin_b, preferred_element_type=jnp.float32)
    im_cos = jnp.einsum("nuv,nv->nu", norm_im, cos_b, preferred_element_type=jnp.float32)
    im_sin = jnp.einsum("nuv,nv->nu", norm_im, sin_b, preferred_element_type=jnp.float32)
    scores = (
        jnp.sum(cos_a * re_cos, 1)
        - jnp.sum(sin_a * re_sin, 1)
        - jnp.sum(sin_a * im_cos, 1)
        - jnp.sum(cos_a * im_sin, 1)
    ) / patch_size
    weights = (0.5 + jax.nn.sigmoid(scores)) * live_mask
    registered = jax.vmap(
        lambda single, shift_down, shift_across: cyclic(
            cyclic(single, shift_down, 0), shift_across, 1
        )
    )(patches, shift_rows, shift_cols)
    contrib = registered.astype(jnp.float32) * weights[:, None, None]
    return (contrib, weights, scores)


def renew(old_rows_all, tile_sums, weight_sums, patch_size):
    totals, weight_all = lax.psum((tile_sums, weight_sums), "tm")
    return (
        (old_rows_all.astype(jnp.float32) + totals)
        / (1.0 + jnp.repeat(weight_all, patch_size))[:, None]
    ).astype(jnp.bfloat16)


def local(frames, offsets, assign, residual, template):
    patch_size = template.shape[2]
    planes_all = template.shape[0]
    grid_rows = template.shape[1] // patch_size
    owners = lax.axis_size("plane")
    plane_dev = frames.shape[1]
    patch_count = plane_dev * grid_rows * owners
    capacity = 2 * patch_count // owners
    plane_group = lax.axis_index("plane")
    cos_t, sin_t = dft_tables(patch_size)
    shifted = jax.vmap(shift_plane)(frames[0], offsets[0])
    patches = to_tiles(shifted, patch_size).reshape(patch_count, patch_size, patch_size)
    owner_col = assign.reshape(patch_count)
    shift_rows = residual[0, :, :, :, 0].reshape(patch_count)
    shift_cols = residual[0, :, :, :, 1].reshape(patch_count)
    counter = jnp.arange(patch_count, dtype=jnp.int32)
    plane_local = counter // (grid_rows * owners)
    row_local = counter // owners % grid_rows
    score_list = []
    column_hit = (owner_col[:, None] == jnp.arange(owners, dtype=jnp.int32)[None, :]).astype(
        jnp.int32
    )
    position = jnp.sum(jnp.cumsum(column_hit, 0) * column_hit, 1) - 1
    slot_index = owner_col * capacity + position
    slot_count = owners * capacity
    placing = slot_index[:, None] == jnp.arange(slot_count, dtype=jnp.int32)[None, :]
    outgoing = jnp.einsum(
        "rs,rxy->sxy", placing.astype(jnp.bfloat16), patches, preferred_element_type=jnp.float32
    ).astype(jnp.bfloat16)
    outgoing = outgoing.reshape(owners, capacity, patch_size, patch_size)
    details = jnp.stack(
        [
            plane_group * plane_dev + plane_local,
            row_local,
            shift_rows,
            shift_cols,
            jnp.ones_like(shift_rows),
        ],
        1,
    )
    outgoing_info = jnp.sum(placing.astype(jnp.int32)[:, :, None] * details[:, None, :], 0).reshape(
        owners, capacity, 5
    )
    current = template
    for round_index in range(ROUNDS):
        tile_stack = current
        temp_re, temp_im = spectrum(tile_stack, cos_t, sin_t)
        arrived = lax.all_to_all(outgoing, "plane", split_axis=0, concat_axis=0, tiled=True)
        arrived_info = lax.all_to_all(
            outgoing_info, "plane", split_axis=0, concat_axis=0, tiled=True
        )
        senders = arrived.shape[0]
        held_slots = arrived.shape[1]
        flat_info = arrived_info.reshape(senders * held_slots, 5)
        target = flat_info[:, 0] * grid_rows + flat_info[:, 1]
        contrib, weights, scores = assess(
            arrived.reshape(senders * held_slots, patch_size, patch_size),
            temp_re[target],
            temp_im[target],
            flat_info[:, 2],
            flat_info[:, 3],
            flat_info[:, 4].astype(jnp.float32),
            cos_t,
            sin_t,
        )
        contrib, weights, scores, target = (
            contrib.reshape(senders, held_slots, patch_size, patch_size),
            weights.reshape(senders, held_slots),
            scores.reshape(senders, held_slots),
            target.reshape(senders, held_slots),
        )
        returned = lax.all_to_all(scores, "plane", split_axis=0, concat_axis=0, tiled=True)
        score_rows = jnp.sum(placing.astype(jnp.float32) * returned.reshape(1, slot_count), 1)
        score_list.append(score_rows.reshape(plane_dev, grid_rows, owners))
        onehot = (
            target.reshape(slot_count)[:, None]
            == jnp.arange(planes_all * grid_rows, dtype=jnp.int32)[None, :]
        ).astype(jnp.float32)
        tile_sums = jnp.einsum(
            "st,sxy->txy",
            onehot,
            contrib.reshape(slot_count, patch_size, patch_size),
            precision=highest,
        )
        weight_sums = jnp.dot(weights.reshape(slot_count), onehot, precision=highest)
        renewed = renew(
            current.reshape(planes_all * grid_rows * patch_size, patch_size),
            tile_sums.reshape(planes_all * grid_rows * patch_size, patch_size),
            weight_sums,
            patch_size,
        )
        current = renewed.reshape(planes_all, grid_rows * patch_size, patch_size)
    return (current, jnp.stack(score_list)[:, None])


REPLICAS = 2
CHUNK = 16 * REPLICAS
MESH = pl.DeviceIdType.MESH


def trig_table(length):
    index = np.arange(length)
    phases = (index[:, None] * index[None, :] % length) * (2.0 * np.pi / length)
    return np.concatenate([np.cos(phases), np.sin(phases)], 1).astype(ml_dtypes.bfloat16)


def mxu(left, right):
    return jnp.dot(left, right, preferred_element_type=jnp.float32)


def wrapped_eye(length, amount, axis):
    near = lax.broadcasted_iota(jnp.int32, (length, length), axis)
    far = lax.broadcasted_iota(jnp.int32, (length, length), 1 - axis)
    return (((near + amount) & (length - 1)) == far).astype(jnp.float32).astype(jnp.bfloat16)


def two_stage(tile, table):
    size = tile.shape[0]
    first = mxu(tile, table)
    first_re = first[:, :size].astype(jnp.bfloat16)
    neg_re = (-first[:, :size]).astype(jnp.bfloat16)
    first_im = (-first[:, size:]).astype(jnp.bfloat16)
    stacked = jnp.concatenate(
        [
            jnp.concatenate([first_re, first_im], 1),
            jnp.concatenate([first_im, neg_re], 1),
        ],
        0,
    )
    return mxu(table, stacked)


def fused_kernel(
    n_tm, cols, plane_dev, offsets_ref, assign_ref, residual_ref, frames_hbm, template_ref, table_hbm,
    out_ref, scores_ref, frames_ref, table_ref, load_s, temp_a, temp_b, reg_src, reg_buf, w_src, w_buf, fin, spec,
    swap_s, swap_r, reg_s, reg_r, w_s, w_r, t_s, t_r, f_s, f_r,
):
    size = table_ref.shape[0]
    chunks = size // CHUNK
    patch_count = plane_dev * cols
    me = lax.axis_index("tm")
    group = lax.axis_index("plane")
    units = n_tm // REPLICAS
    unit = lax.rem(me, units)
    base = me - unit
    flat = unit * cols + group
    assigned = [assign_ref[q // cols, 0, q % cols] for q in range(patch_count)]
    down = [residual_ref[q // cols, q % cols, 0] for q in range(patch_count)]
    across_by = [residual_ref[q // cols, q % cols, 1] for q in range(patch_count)]

    def place(owner):
        owner = lax.rem(owner, units)
        plane = lax.div(owner, chunks)
        row = pl.multiple_of(lax.rem(owner, chunks) * CHUNK, CHUNK)
        return plane, pl.ds(row, CHUNK)

    my_plane, my_rows = place(me)

    def around(body):
        def step(r, carry):
            body(lax.rem(me + r, n_tm))
            return carry

        lax.fori_loop(1, n_tm, step, 0)

    def replica(body):
        def step(r, carry):
            body(lax.rem(unit + r, units))
            return carry

        lax.fori_loop(1, units, step, 0)

    def owners_of(plane, first, count, body):
        def step(r, carry):
            owner = plane * chunks + lax.rem(unit + r, chunks)
            for part in range(count):
                device = first + part * units + owner
                pl.when(device != me)(functools.partial(body, device))
            return carry

        lax.fori_loop(0, chunks, step, 0)

    def across(body):
        def step(r, carry):
            body(lax.rem(group + r, cols))
            return carry

        lax.fori_loop(1, cols, step, 0)

    def everyone(body):
        def step(r, carry):
            other = lax.rem(flat + r, units * cols)
            body(other, lax.div(other, cols), lax.rem(other, cols))
            return carry

        lax.fori_loop(1, units * cols, step, 0)

    frames_load = pltpu.make_async_copy(frames_hbm.at[0], frames_ref, load_s.at[0])
    table_load = pltpu.make_async_copy(table_hbm, table_ref, load_s.at[1])
    own_load = pltpu.make_async_copy(
        template_ref.at[pl.ds(group * plane_dev, plane_dev)], temp_a.at[group], load_s.at[2]
    )
    frames_load.start()
    table_load.start()
    own_load.start()

    barrier = pltpu.get_barrier_semaphore()
    around(
        lambda j: pl.semaphore_signal(barrier, inc=1, device_id=(j, group), device_id_type=MESH)
    )
    across(lambda h: pl.semaphore_signal(barrier, inc=1, device_id=(me, h), device_id_type=MESH))

    frames_load.wait()

    patches = []
    for plane in range(plane_dev):
        frame = frames_ref[plane]
        rows = mxu(wrapped_eye(size, offsets_ref[plane, 0], 0), frame).astype(jnp.bfloat16)
        shifted = mxu(
            rows, wrapped_eye(frame.shape[1], offsets_ref[plane, 1], 1)
        ).astype(jnp.bfloat16)
        for col in range(cols):
            patches.append(shifted[:, col * size : (col + 1) * size])
    for q, patch in enumerate(patches):
        rolled = mxu(wrapped_eye(size, down[q], 0), patch).astype(jnp.bfloat16)
        rolled = mxu(rolled, wrapped_eye(size, across_by[q], 1))
        reg_src[q // cols, q % cols] = rolled.astype(jnp.bfloat16)

    pl.semaphore_wait(barrier, n_tm - 1 + cols - 1)

    def swap_copy(to, slot):
        return pltpu.make_async_remote_copy(
            src_ref=template_ref.at[pl.ds(to * plane_dev, plane_dev)],
            dst_ref=temp_a.at[slot],
            send_sem=swap_s.at[to],
            recv_sem=swap_r.at[slot],
            device_id=(me, to),
            device_id_type=MESH,
        )

    def reg_copy(to, slot):
        plane, rows = place(to)
        return pltpu.make_async_remote_copy(
            src_ref=reg_src.at[plane, :, rows, :],
            dst_ref=reg_buf.at[slot],
            send_sem=reg_s.at[to],
            recv_sem=reg_r.at[slot],
            device_id=(to, group),
            device_id_type=MESH,
        )

    def w_copy(k, to, slot):
        return pltpu.make_async_remote_copy(
            src_ref=w_src.at[k, lax.div(lax.rem(to, units), chunks)],
            dst_ref=w_buf.at[k, slot],
            send_sem=w_s.at[k, to],
            recv_sem=w_r.at[k, slot],
            device_id=(to, group),
            device_id_type=MESH,
        )

    def t_copy(to, owner):
        plane, rows = place(owner)
        return pltpu.make_async_remote_copy(
            src_ref=temp_b.at[:, plane, rows, :],
            dst_ref=temp_b.at[:, plane, rows, :],
            send_sem=t_s.at[to],
            recv_sem=t_r.at[owner],
            device_id=(base + to, group),
            device_id_type=MESH,
        )

    def f_copy(to, to_tm, to_plane, owner, owner_tm, owner_plane):
        plane, rows = place(owner_tm)
        return pltpu.make_async_remote_copy(
            src_ref=fin.at[to_plane],
            dst_ref=out_ref.at[owner_plane * plane_dev + plane, rows, :],
            send_sem=f_s.at[to],
            recv_sem=f_r.at[owner],
            device_id=(base + to_tm, to_plane),
            device_id_type=MESH,
        )

    across(lambda h: swap_copy(h, group).start())
    around(lambda j: reg_copy(j, me).start())
    reg_buf[me] = reg_src[my_plane, :, my_rows, :]
    table_load.wait()
    table = table_ref[...].astype(jnp.bfloat16)
    for q, patch in enumerate(patches):
        spec[q] = two_stage(patch, table)

    row_id = lax.broadcasted_iota(jnp.int32, (2 * patch_count, size), 0)
    lane_id = lax.broadcasted_iota(jnp.int32, (2 * patch_count, size), 1)
    wanted = jnp.zeros((2 * patch_count, size), jnp.int32)
    for q in range(patch_count):
        wanted = jnp.where(row_id == q, down[q], wanted)
        wanted = jnp.where(row_id == patch_count + q, across_by[q], wanted)
    onehot = ((wanted & (size - 1)) == lane_id).astype(jnp.float32).astype(jnp.bfloat16)
    picked = mxu(onehot, table)
    left = jnp.concatenate(
        [picked[:patch_count, :size], picked[:patch_count, size:]], 0
    ).astype(jnp.bfloat16)

    own_load.wait()
    across(lambda h: swap_copy(h, h).wait_recv())

    lane_at = lax.broadcasted_iota(jnp.int32, (1, size), 1)
    for k in range(ROUNDS):
        temp = temp_a if k == 0 else temp_b
        for q in range(patch_count):
            plane, col = q // cols, q % cols
            if col == 0:
                score_row = jnp.zeros((1, size), jnp.float32)
                weight_row = jnp.zeros((1, size), jnp.float32)
                if k > 0:
                    owners_of(plane, base, 1, lambda j: t_copy(j - base, j - base).wait_recv())
            target = jnp.full((size, size), assigned[q], jnp.int32)
            tile = temp[0, plane].astype(jnp.float32)
            for c in range(1, cols):
                tile = jnp.where(target == c, temp[c, plane].astype(jnp.float32), tile)
            temp_spec = two_stage(tile.astype(jnp.bfloat16), table)
            temp_re, temp_im = temp_spec[:, :size], temp_spec[:, size:]
            patch_re, patch_im = spec[q, :, :size], spec[q, :, size:]
            cross_re = patch_re * temp_re + patch_im * temp_im
            cross_im = patch_im * temp_re - patch_re * temp_im
            modulus = jnp.sqrt(cross_re * cross_re + cross_im * cross_im)
            level = jnp.sum(modulus, axis=0, keepdims=True)
            level = jnp.sum(level, axis=1, keepdims=True) * (1.0 / (size * size))
            inverse = 1.0 / (modulus + (0.1 * level + 1e-06))
            norm = jnp.concatenate(
                [
                    (cross_re * inverse).astype(jnp.bfloat16),
                    (cross_im * inverse).astype(jnp.bfloat16),
                ],
                1,
            )
            summed = mxu(left, norm)
            cos_row = summed[q : q + 1]
            sin_row = summed[patch_count + q : patch_count + q + 1]
            cos_b = picked[patch_count + q : patch_count + q + 1, :size]
            sin_b = picked[patch_count + q : patch_count + q + 1, size:]
            terms = (cos_row[:, :size] - sin_row[:, size:]) * cos_b - (
                sin_row[:, :size] + cos_row[:, size:]
            ) * sin_b
            score = jnp.sum(terms, axis=1, keepdims=True) * (1.0 / size)
            score = jnp.broadcast_to(score, (8, size))[:1]
            score_row = jnp.where(lane_at == col, score, score_row)
            weight = 1.0 + 0.5 * jnp.tanh(0.5 * score)
            target_row = jnp.full((1, size), assigned[q], jnp.int32)
            weight_row = jnp.where(lane_at == col * cols + target_row, weight, weight_row)
            if col == cols - 1:
                w_src[k, plane] = weight_row
                owners_of(plane, 0, REPLICAS, lambda j: w_copy(k, j, me).start())
                scores_ref[k, 0, plane] = score_row[:, :cols]
        w_buf[k, me] = w_src[k, my_plane]
        if k == 0:
            around(lambda j: reg_copy(j, j).wait_recv())
        around(lambda j: w_copy(k, j, j).wait_recv())

        sums = [temp[c, my_plane, my_rows, :].astype(jnp.float32) for c in range(cols)]
        lanes = lax.broadcasted_iota(jnp.int32, (n_tm, size), 1)
        gathered = w_buf[k].reshape(n_tm, size)
        spread = [
            jnp.broadcast_to(
                jnp.sum(jnp.where(lanes == row, gathered, 0.0), axis=1, keepdims=True),
                (n_tm, size),
            )
            for row in range(cols * cols)
        ]
        for v in range(n_tm):
            for c2 in range(cols):
                piece = reg_buf[v, c2].astype(jnp.float32)
                for c in range(cols):
                    sums[c] = sums[c] + piece * spread[c2 * cols + c][v : v + 1]
        for c in range(cols):
            weights = spread[c]
            for c2 in range(1, cols):
                weights = weights + spread[c2 * cols + c]
            total = 1.0 + jnp.sum(weights, axis=0, keepdims=True)
            fresh = (sums[c] / total).astype(jnp.bfloat16)
            if k < ROUNDS - 1:
                temp_b[c, my_plane, my_rows, :] = fresh
            else:
                fin[c] = fresh
        if k < ROUNDS - 1:
            replica(lambda u: t_copy(u, unit).start())

    everyone(lambda d, j, h: f_copy(d, j, h, flat, unit, group).start())
    own_store = pltpu.make_async_copy(
        fin.at[group], out_ref.at[group * plane_dev + my_plane, my_rows, :], load_s.at[3]
    )
    own_store.start()
    across(lambda h: swap_copy(h, group).wait_send())
    around(lambda j: reg_copy(j, me).wait_send())
    for k in range(ROUNDS):
        around(lambda j: w_copy(k, j, me).wait_send())
    replica(lambda u: t_copy(u, unit).wait_send())
    own_store.wait()
    everyone(lambda d, j, h: f_copy(d, j, h, d, j, h).wait_recv())
    everyone(lambda d, j, h: f_copy(d, j, h, flat, unit, group).wait_send())


def handing_on_kernel(
    parts, template_in, scores_in, template_out, scores_out, template_mid, scores_mid, load, store
):
    rows = template_in.shape[0] // parts
    moves = [(scores_in, scores_mid, scores_out)]
    for part in range(parts):
        here = pl.ds(part * rows, rows)
        moves.append((template_in.at[here], template_mid.at[here], template_out.at[here]))
    loads = [
        pltpu.make_async_copy(source, middle, load.at[i])
        for i, (source, middle, _) in enumerate(moves)
    ]
    stores = [
        pltpu.make_async_copy(middle, target, store.at[i])
        for i, (_, middle, target) in enumerate(moves)
    ]
    for copy in loads:
        copy.start()
    for arrival, departure in zip(loads, stores):
        arrival.wait()
        departure.start()
    for copy in stores:
        copy.wait()


def handing_on(template, scores):
    parts = template.shape[0]
    hbm = pl.BlockSpec(memory_space=pltpu.HBM)
    return pl.pallas_call(
        functools.partial(handing_on_kernel, parts),
        out_shape=(
            jax.ShapeDtypeStruct(template.shape, template.dtype),
            jax.ShapeDtypeStruct(scores.shape, scores.dtype),
        ),
        in_specs=[hbm, hbm],
        out_specs=(hbm, hbm),
        scratch_shapes=[
            pltpu.VMEM(template.shape, template.dtype),
            pltpu.VMEM(scores.shape, scores.dtype),
            pltpu.SemaphoreType.DMA((parts + 1,)),
            pltpu.SemaphoreType.DMA((parts + 1,)),
        ],
    )(template, scores)


def fused(n_tm, cols, frames, offsets, assign, residual, template):
    plane_dev = frames.shape[1]
    size = template.shape[2]
    patch_count = plane_dev * cols
    vmem = pl.BlockSpec(memory_space=pltpu.VMEM)
    smem = pl.BlockSpec(memory_space=pltpu.SMEM)
    hbm = pl.BlockSpec(memory_space=pltpu.HBM)
    dma = pltpu.SemaphoreType.DMA
    return pl.pallas_call(
        functools.partial(fused_kernel, n_tm, cols, plane_dev),
        out_shape=(
            jax.ShapeDtypeStruct(template.shape, jnp.bfloat16),
            jax.ShapeDtypeStruct((ROUNDS, 1, plane_dev, 1, cols), jnp.float32),
        ),
        in_specs=[smem, smem, smem, hbm, hbm, hbm],
        out_specs=(hbm, vmem),
        scratch_shapes=[
            pltpu.VMEM(frames.shape[1:], jnp.bfloat16),
            pltpu.VMEM((size, 2 * size), jnp.float32),
            dma((4,)),
            pltpu.VMEM((cols, plane_dev, size, size), jnp.bfloat16),
            pltpu.VMEM((cols, plane_dev, size, size), jnp.bfloat16),
            pltpu.VMEM((plane_dev, cols, size, size), jnp.bfloat16),
            pltpu.VMEM((n_tm, cols, CHUNK, size), jnp.bfloat16),
            pltpu.VMEM((ROUNDS, plane_dev, 1, size), jnp.float32),
            pltpu.VMEM((ROUNDS, n_tm, 1, size), jnp.float32),
            pltpu.VMEM((cols, CHUNK, size), jnp.bfloat16),
            pltpu.VMEM((patch_count, size, 2 * size), jnp.float32),
            dma((cols,)),
            dma((cols,)),
            dma((n_tm,)),
            dma((n_tm,)),
            dma((ROUNDS, n_tm)),
            dma((ROUNDS, n_tm)),
            dma((n_tm // REPLICAS,)),
            dma((n_tm // REPLICAS,)),
            dma((n_tm // REPLICAS * cols,)),
            dma((n_tm // REPLICAS * cols,)),
        ],
        compiler_params=pltpu.CompilerParams(
            collective_id=0, has_side_effects=True
        ),
    )(
        offsets.reshape(plane_dev, 2),
        assign.reshape(plane_dev, 1, cols),
        residual.reshape(plane_dev, cols, 2),
        frames,
        template,
        jnp.asarray(trig_table(size).astype(np.float32)),
    )


def dispatch(n_tm, cols, frames, offsets, assign, residual, template):
    size = template.shape[2]
    plane_dev = frames.shape[1]
    width = frames.shape[3]
    fits = (
        n_tm % REPLICAS == 0
        and plane_dev * size == n_tm // REPLICAS * CHUNK
        and template.shape[1] == size
        and cols * cols <= 8
        and 2 * plane_dev * cols <= 8
        and size & (size - 1) == 0
        and width & (width - 1) == 0
        and size % 128 == 0
    )
    if fits:
        return handing_on(*fused(n_tm, cols, frames, offsets, assign, residual, template))
    return local(frames, offsets, assign, residual, template)


def solution(mesh):
    return jax.shard_map(
        functools.partial(dispatch, mesh.shape["tm"], mesh.shape["plane"]),
        mesh=mesh,
        in_specs=(
            P("tm", "plane", None, None),
            P("tm", "plane", None),
            P("tm", "plane", None, None, None),
            P("tm", "plane", None, None, None),
            P(None, None, "plane"),
        ),
        out_specs=(P(None, None, "plane"), P(None, "tm", "plane", None, None)),
        check_vma=False,
    )
```
